256 devices in a mesh: inst: 16 (over y, x_lo, core), tp: 16 (over x_hi, z).
Axes of the slice: x: 4 (x_hi: 2, x_lo: 2; x = x_hi * 2 + x_lo), y: 4, z: 8, core: 2. Of those that a mesh axis runs over, the one named last changes fastest.
Arguments:
- source_cache: bfloat16 [16, 16, 2, 512, 1024], P('inst', 'tp'), may hold values from -6 to 6
- resident_cache: bfloat16 [16, 16, 8, 2, 512, 128], P('inst', 'tp'), may hold values from -6 to 6
- new_kv: bfloat16 [16, 24, 2, 1024], P('inst'), may hold values from -6 to 6
- queries: bfloat16 [16, 24, 4096], P('inst', None, 'tp'), may hold values from -103 to 103
- residual: bfloat16 [16, 24, 8192], P('inst'), may hold values from -1.5 to 1.5
- lengths: int32 [16, 24], P('inst'), may hold values from 1 to 512, 6144 in all within a row
- out_weight: bfloat16 [4096, 8192], P('tp'), may hold values from -0.09375 to 0.09375
Outputs:
- mixed: bfloat16 [16, 24, 8192], P('inst')
- adopted_cache: bfloat16 [16, 16, 16, 2, 512, 128], P('inst', 'tp')
The draws below stay inside these ranges and needn't reach their ends.
All inputs are finite; a program needn't handle non-finite values.
Results may differ from the reference program's by a relative error of at most 0.0052.
Values may be sent and summed in bfloat16 or wider, within the bound.
No kernel may reach another device: no remote copies, remote signals or barrier semaphores. Data moves between devices by JAX's collectives and lax.ppermute only.
A program may use at most 64 MiB of HBM per device.

```python
import math
import jax
import jax.numpy as jnp
import numpy as np
from jax import lax

D = 8192
HD = 128
KVH = 8
QH = 32
LEN = 512
RES = 8
ADOPT = 16
ROWS = 24
KV_DEV = 1
N_INST = 16
N_TP = 16


def draw_queries(key, part):
    key = jax.random.fold_in(key, 7)
    first_key = jax.random.fold_in(key, 0)
    values = jnp.clip(2.0 * jax.random.normal(first_key, (N_INST, ROWS, QH * HD), jnp.float32), -12.0, 12.0)
    return values.astype(jnp.bfloat16)


def block_scale(rng, extent, pieces, least, top_value):
    gain, own = 1.0, jax.random.fold_in(rng, 6)
    for dim, blocks in pieces:
        steps = jnp.exp(jax.random.uniform(jax.random.fold_in(own, dim), (blocks,), jnp.float32, least / len(pieces), top_value / len(pieces)))
        gain = gain * jnp.repeat(steps, extent[dim] // blocks).reshape([-1 if axis == dim else 1 for axis in range(len(extent))])
    return gain


def split_up(number_of, total, bound, skew):
    weights = [(1 << 20) // math.isqrt(grade ** skew) + 1 for grade in range(2, number_of + 1)]
    rest, counts = total - bound - (number_of - 1), [1] * (number_of - 1)
    while rest > 0:
        free = [i for i in range(number_of - 1) if counts[i] < bound]
        whole, remaining = sum([weights[i] for i in free]), rest
        for i in free:
            more = min(bound - counts[i], max(1, remaining * weights[i] // whole), rest)
            counts[i] = counts[i] + more
            rest = rest - more
    return np.array([bound] + counts)


def uneven_parts(own_key, count, total, limit, slope):
    if count == 2:
        one = jax.random.randint(own_key, (), max(1, total - limit), min(limit, total - 1) + 1)
        return jnp.stack([one, total - one])
    sizes = jnp.asarray(split_up(count, total, limit, slope), jnp.int32)
    twos = (count - 1) // 2
    giver, taker = sizes[1:1 + 2 * twos:2], sizes[2:2 + 2 * twos:2]
    slack = jnp.minimum(giver - 1, limit - taker)
    shifted = jax.random.randint(jax.random.fold_in(own_key, 1), (twos,), 0, 1 << 20) % (slack + 1)
    sizes = sizes.at[1:1 + 2 * twos:2].set(giver - shifted).at[2:2 + 2 * twos:2].set(taker + shifted)
    return sizes[jax.random.permutation(jax.random.fold_in(own_key, 2), count)]


def centred(stream_key, dims, spread, limit, pieces=(), kind=jnp.bfloat16):
    entries = jax.random.normal(stream_key, dims, jnp.float32) * spread
    if len(pieces) > 0:
        entries = block_scale(stream_key, dims, pieces, -0.22, 0.18) * entries
    return jnp.clip(entries, min=-limit, max=limit).astype(kind)


def setup_inputs(seed: int = 0) -> dict:
    splits = jax.random.split(jax.random.key(seed), 8)
    source_cache = centred(splits[0], (N_INST, ADOPT, 2, LEN, KVH * HD), 1.0, 6.0, ((0, 16), (1, 16)))
    resident_cache = centred(splits[1], (N_INST, N_TP, RES, 2, LEN, KV_DEV * HD), 1.0, 6.0, ((0, 16), (1, 16)))
    new_kv = centred(splits[2], (N_INST, ROWS, 2, KVH * HD), 1.0, 6.0, ((0, 16),))
    queries = draw_queries(jax.random.fold_in(splits[7], 71), 0)
    residual = centred(splits[4], (N_INST, ROWS, D), 0.25, 1.5, ((0, 16),))
    lengths = jax.vmap(lambda own: uneven_parts(own, ROWS, ROWS * LEN // 2, LEN, 1))(jax.random.split(splits[5], N_INST)).reshape((N_INST, ROWS)).astype(jnp.int32)
    out_weight = centred(splits[6], (QH * HD, D), (QH * HD) ** -0.5, 0.09375, ((0, 16),))
    return dict(source_cache=source_cache, resident_cache=resident_cache, new_kv=new_kv, queries=queries, residual=residual, lengths=lengths, out_weight=out_weight)


def attend(query_vector, key_cache, value_cache, incoming_key, value_fresh, seq_lengths):
    softmax_scale = 1.0 / math.sqrt(query_vector.shape[-1])
    query_broadcast = query_vector.astype(jnp.float32)
    scores = jnp.einsum('bkgd,blkd->bkgl', query_broadcast, key_cache.astype(jnp.float32)) * softmax_scale
    local_score = jnp.einsum('heox,hex->heo', query_broadcast, incoming_key.astype(jnp.float32)) * softmax_scale
    places = jnp.arange(key_cache.shape[1], dtype=jnp.int32)
    live_mask = (places[None, :] < seq_lengths[:, None])[:, None, None, :]
    scores = jnp.where(live_mask, scores, -1e+30)
    top_score = jnp.maximum(lax.optimization_barrier(jnp.max(scores, axis=-1)), local_score)
    weights = jnp.where(live_mask, jnp.exp(scores - top_score[..., None]), 0.0)
    local_weight = jnp.exp(local_score - top_score)
    total = lax.optimization_barrier(jnp.sum(weights, axis=-1)) + local_weight
    probs = lax.optimization_barrier((weights / total[..., None]).astype(jnp.bfloat16))
    own_prob = lax.optimization_barrier((local_weight / total).astype(jnp.bfloat16))
    blended = jnp.einsum('bkgl,blkd->bkgd', probs.astype(jnp.float32), value_cache.astype(jnp.float32))
    blended = blended + own_prob.astype(jnp.float32)[..., None] * value_fresh.astype(jnp.float32)[:, :, None, :]
    return blended.reshape(blended.shape[0], -1).astype(jnp.bfloat16)

def reference(source_cache, resident_cache, new_kv, queries, residual, lengths, out_weight):
    half_way = N_INST // 2
    handed = jnp.roll(source_cache, half_way, axis=0)
    handed_len = jnp.roll(lengths[:, :ADOPT], half_way, axis=0)
    own_len = lengths[:, ADOPT:]
    group = QH // KVH
    per_dev = QH // N_TP
    kv_dev = max(1, per_dev // group)
    per_kv = per_dev // kv_dev
    head_table = np.array([[dev * per_dev // group + slot for slot in range(kv_dev)] for dev in range(N_TP)], dtype=np.int32)
    split_heads = handed.reshape(N_INST, ADOPT, 2, LEN, KVH, HD)[:, :, :, :, head_table]
    adopted_cache = jnp.transpose(split_heads, (0, 4, 1, 2, 3, 5, 6)).reshape(N_INST, N_TP, ADOPT, 2, LEN, kv_dev * HD)

    def one_instance(items):
        cache, resident, fresh, query_vector, resid, res_len, hand_len = items
        fresh = fresh.reshape(ROWS, 2, KVH, HD)
        query_heads = query_vector.reshape(ROWS, QH, HD)
        query_adopt = query_heads[:ADOPT].reshape(ADOPT, KVH, group, HD)
        cache_heads = cache.reshape(ADOPT, 2, LEN, KVH, HD)
        out_adopt = attend(query_adopt, cache_heads[:, 0], cache_heads[:, 1], fresh[:ADOPT, 0], fresh[:ADOPT, 1], hand_len)
        query_res = query_heads[ADOPT:].reshape(RES * N_TP, kv_dev, per_kv, HD)
        resident_rows = jnp.transpose(resident, (1, 0, 2, 3, 4)).reshape(RES * N_TP, 2, LEN, kv_dev, HD)
        fresh_res = fresh[ADOPT:][:, :, head_table]
        fresh_res = jnp.transpose(fresh_res, (0, 2, 1, 3, 4)).reshape(RES * N_TP, 2, kv_dev, HD)
        out_res = attend(query_res, resident_rows[:, 0], resident_rows[:, 1], fresh_res[:, 0], fresh_res[:, 1], jnp.repeat(res_len, N_TP))
        out_res = out_res.reshape(RES, QH * HD)
        attn = jnp.concatenate([out_adopt, out_res], axis=0)
        value_portion = jnp.dot(attn, out_weight, preferred_element_type=jnp.float32)
        return (resid.astype(jnp.float32) + value_portion).astype(jnp.bfloat16)
    mixed = lax.map(one_instance, (handed, resident_cache, new_kv, queries, residual, own_len, handed_len))
    return (mixed, adopted_cache)
```

```python
import functools
import math

import jax
import jax.numpy as jnp
import numpy as np
from jax import lax
from jax.experimental import pallas as pl
from jax.experimental.pallas import tpu as pltpu
from jax.sharding import PartitionSpec as P

HD = 128
KVH = 8
QH = 32
GROUP = QH // KVH
NZ = 8
PAD = 8
MIB = 1 << 20
ROUNDS = ((-3, 0), (0, 1), (2, 0), (-1, 1), (-3, 1), (0, 0), (2, 1), (-1, 0))
N_ROUNDS = len(ROUNDS)

ANY = pl.BlockSpec(memory_space=pl.ANY)
VMEM = pl.BlockSpec(memory_space=pltpu.VMEM)
SMEM = pl.BlockSpec(memory_space=pltpu.SMEM)


def round_target(rank, step):
    shift, flip = ROUNDS[step]
    high, low = divmod(rank, NZ)
    sign = 1 if low % 2 == 0 else -1
    return (high + flip) % 2 * NZ + (low + sign * shift) % NZ


def partner(rank):
    return rank ^ 1


def tables(count, rows):
    heads = np.zeros((count, N_ROUNDS), np.int32)
    mine = np.zeros((count, N_ROUNDS), np.int32)
    for rank in range(count):
        for step in range(N_ROUNDS):
            target = round_target(rank, step)
            heads[rank, step] = target // 2
            mine[target, step] = rank
    theirs = mine[[partner(rank) for rank in range(count)]]
    late = np.broadcast_to(np.arange(count, rows, dtype=np.int32), (count, rows - count))
    order = np.concatenate([mine, theirs, late], axis=1)
    place = np.arange(rows)[None, :, None] == order[:, None, :]
    select = np.concatenate([mine, late], axis=1)[:, :, None] == np.arange(rows)[None, None, :]
    return np.concatenate([heads, mine, theirs], axis=1), place, select


def run_copies(copies):
    for copy in copies:
        copy.start()
    for copy in copies:
        copy.wait()


def extract_kernel(index_ref, cache_ref, *rest):
    outs, sem = rest[:N_ROUNDS], rest[N_ROUNDS]
    copies = []
    for step in range(N_ROUNDS):
        columns = pl.ds(pl.multiple_of(index_ref[step] * HD, HD), HD)
        copies.append(pltpu.make_async_copy(cache_ref.at[:, :, columns], outs[step], sem.at[step]))
    run_copies(copies)


def extract(index, cache):
    shape = jax.ShapeDtypeStruct((2, cache.shape[1], HD), cache.dtype)
    return pl.pallas_call(
        extract_kernel,
        out_shape=[shape] * N_ROUNDS,
        in_specs=[SMEM, ANY],
        out_specs=[VMEM] * N_ROUNDS,
        scratch_shapes=[pltpu.SemaphoreType.DMA((N_ROUNDS,))],
        compiler_params=pltpu.CompilerParams(vmem_limit_bytes=16 * MIB),
        name="extract",
    )(index, cache)


def place_kernel(offset, count, has_base, index_ref, *rest):
    blocks = rest[:count]
    out_ref, sem = rest[count + has_base], rest[count + has_base + 1]
    run_copies([
        pltpu.make_async_copy(blocks[i], out_ref.at[index_ref[offset + i]], sem.at[i])
        for i in range(count)
    ])


def place(index, offset, blocks, rows, base=None):
    count = len(blocks)
    has_base = 0 if base is None else 1
    extra = [] if base is None else [base]
    return pl.pallas_call(
        functools.partial(place_kernel, offset, count, has_base),
        out_shape=jax.ShapeDtypeStruct((rows,) + blocks[0].shape, blocks[0].dtype),
        in_specs=[SMEM] + [VMEM] * count + [ANY] * has_base,
        out_specs=ANY,
        scratch_shapes=[pltpu.SemaphoreType.DMA((count,))],
        input_output_aliases={1 + count: 0} if has_base else {},
        compiler_params=pltpu.CompilerParams(vmem_limit_bytes=16 * MIB),
        name="place",
    )(index, *blocks, *extra)


def attend_kernel(first, heads, scale, len_ref, rows_ref, *rest):
    n_out = heads // 2
    blocks, outs = rest[: -5 - n_out], rest[-5 - n_out : -5]
    q_ref, k_ref, v_ref, prob_ref, blend_ref = rest[-5:]
    count = q_ref.shape[0] // PAD

    def block(b, kind):
        return blocks[0][b, kind] if len(blocks) == 1 else blocks[b][kind]

    new = GROUP * HD
    picked = slice(first, first + count)
    for g in range(PAD):
        spread = pl.ds(g, count, stride=PAD)
        lane = min(g, heads - 1) * HD
        q_ref[spread, :] = rows_ref[picked, lane : lane + HD]
        k_ref[spread, :] = rows_ref[picked, new : new + HD]
        v_ref[spread, :] = rows_ref[picked, new + HD : new + 2 * HD]
    for b in range(count):
        rows = slice(b * PAD, (b + 1) * PAD)
        scores = lax.dot_general(
            q_ref[rows, :].astype(jnp.bfloat16),
            block(b, 0),
            (((1,), (1,)), ((), ())),
            preferred_element_type=jnp.float32,
        )
        live = lax.broadcasted_iota(jnp.int32, scores.shape, 1) < len_ref[b]
        prob_ref[rows, :] = jnp.where(live, scores * scale, -1e30)
    scores = prob_ref[...]
    own = jnp.sum(q_ref[...] * k_ref[...], axis=-1, keepdims=True) * scale
    top = jnp.maximum(jnp.max(scores, axis=-1, keepdims=True), own)
    weights = jnp.exp(scores - top)
    own_weight = jnp.exp(own - top)
    total = jnp.sum(weights, axis=-1, keepdims=True) + own_weight
    prob_ref[...] = weights / total
    own_prob = (own_weight / total).astype(jnp.bfloat16).astype(jnp.float32)
    fresh = own_prob * v_ref[...]
    for b in range(count):
        rows = slice(b * PAD, (b + 1) * PAD)
        blended = jnp.dot(
            prob_ref[rows, :].astype(jnp.bfloat16),
            block(b, 1),
            preferred_element_type=jnp.float32,
        )
        blend_ref[rows, :] = blended + fresh[rows, :]
    for g in range(heads):
        outs[g // 2][:, g % 2 * HD : (g % 2 + 1) * HD] = blend_ref[pl.ds(g, count, stride=PAD), :]


def attend(first, heads, lengths, table, blocks):
    span = blocks[0].shape[-2]
    count = lengths.shape[0]
    wide = pltpu.VMEM((count * PAD, HD), jnp.float32)
    return pl.pallas_call(
        functools.partial(attend_kernel, first, heads, 1.0 / math.sqrt(HD)),
        out_shape=[jax.ShapeDtypeStruct((count, 2 * HD), jnp.float32)] * (heads // 2),
        in_specs=[SMEM] + [VMEM] * (1 + len(blocks)),
        out_specs=[VMEM] * (heads // 2),
        scratch_shapes=[wide, wide, wide, pltpu.VMEM((count * PAD, span), jnp.float32), wide],
        compiler_params=pltpu.CompilerParams(vmem_limit_bytes=16 * MIB),
        name="attend",
    )(lengths, table, *blocks)


def project_kernel(place_ref, kept_ref, traded_ref, res_ref, weight_ref, out_ref):
    gathered = jnp.concatenate([kept_ref[...], traded_ref[...], res_ref[...]], axis=0)
    attn = jnp.dot(
        place_ref[...], gathered.astype(jnp.bfloat16), preferred_element_type=jnp.float32
    ).astype(jnp.bfloat16)
    chunk = out_ref.shape[2]
    for c in range(out_ref.shape[0]):
        out_ref[c] = jnp.dot(
            attn, weight_ref[:, c * chunk : (c + 1) * chunk], preferred_element_type=jnp.float32
        ).astype(out_ref.dtype)


def project(order, kept, traded, res, weight, count):
    rows = order.shape[0]
    return pl.pallas_call(
        project_kernel,
        out_shape=jax.ShapeDtypeStruct((count, rows, weight.shape[1] // count), jnp.bfloat16),
        in_specs=[VMEM] * 5,
        out_specs=VMEM,
        compiler_params=pltpu.CompilerParams(vmem_limit_bytes=24 * MIB),
        name="project",
    )(order, kept, traded, res, weight)


def total_kernel(parts_ref, residual_ref, out_ref):
    summed = parts_ref[0].astype(jnp.float32)
    for c in range(1, parts_ref.shape[0]):
        summed = summed + parts_ref[c].astype(jnp.float32)
    mixed = (residual_ref[...].astype(jnp.float32) + summed).astype(out_ref.dtype)
    for c in range(out_ref.shape[0]):
        out_ref[c] = mixed


def total(parts, residual):
    return pl.pallas_call(
        total_kernel,
        out_shape=jax.ShapeDtypeStruct(parts.shape, jnp.bfloat16),
        in_specs=[VMEM] * 2,
        out_specs=VMEM,
        compiler_params=pltpu.CompilerParams(vmem_limit_bytes=16 * MIB),
        name="total",
    )(parts, residual)


def join_kernel(parts_ref, out_ref):
    chunk = parts_ref.shape[2]
    for c in range(parts_ref.shape[0]):
        out_ref[0, :, c * chunk : (c + 1) * chunk] = parts_ref[c]


def join(parts):
    count, rows, chunk = parts.shape
    return pl.pallas_call(
        join_kernel,
        out_shape=jax.ShapeDtypeStruct((1, rows, count * chunk), parts.dtype),
        in_specs=[VMEM],
        out_specs=VMEM,
        compiler_params=pltpu.CompilerParams(vmem_limit_bytes=16 * MIB),
        name="join",
    )(parts)


def hop(value, inst_count, tp_count, target):
    half = inst_count // 2
    pairs = [
        (i * tp_count + t, (i + half) % inst_count * tp_count + target(t))
        for i in range(inst_count)
        for t in range(tp_count)
    ]
    return lax.ppermute(value, ("inst", "tp"), pairs)


def swap(value, tp_count):
    return lax.ppermute(value, "tp", [(t, partner(t)) for t in range(tp_count)])


def on_device(source_cache, resident_cache, new_kv, queries, residual, lengths, out_weight):
    tp_count = lax.axis_size("tp")
    inst_count = lax.axis_size("inst")
    rank = lax.axis_index("tp")
    rows = queries.shape[1]
    adopt = tp_count
    chunk = out_weight.shape[1] // tp_count

    index, order, select = tables(tp_count, rows)
    index = lax.dynamic_index_in_dim(jnp.asarray(index), rank, keepdims=False)
    order = lax.dynamic_index_in_dim(jnp.asarray(order, jnp.bfloat16), rank, keepdims=False)
    select = lax.dynamic_index_in_dim(jnp.asarray(select, jnp.bfloat16), rank, keepdims=False)
    mine = index[N_ROUNDS : 2 * N_ROUNDS]

    handed = hop(lengths[0], inst_count, tp_count, lambda t: t)
    other_q = swap(queries[0], tp_count)
    sent = extract(index, source_cache[0, 0])
    arrived = [
        hop(sent[step], inst_count, tp_count, lambda t, step=step: round_target(t, step))
        for step in range(N_ROUNDS)
    ]
    passed = [swap(block, tp_count) for block in arrived]

    fresh = lax.dynamic_slice_in_dim(new_kv[0], rank // 2 * HD, HD, axis=2)
    table = jnp.concatenate([queries[0], other_q, fresh.reshape(rows, 2 * HD)], axis=1)
    table = jnp.dot(select, table, preferred_element_type=jnp.float32)
    hit = mine[:, None] == jnp.arange(rows, dtype=jnp.int32)[None, :]
    adopt_len = jnp.sum(jnp.where(hit, handed[None, :], 0), axis=1)
    (res,) = attend(N_ROUNDS, 2, lengths[0, adopt:], table, [resident_cache[0, 0]])
    kept, traded = attend(0, GROUP, adopt_len, table, arrived)
    traded = swap(traded, tp_count)

    parts = project(order, kept, traded, res, out_weight, tp_count)
    parts = lax.all_to_all(parts, "tp", 0, 0)
    own_residual = lax.dynamic_slice_in_dim(residual[0], rank * chunk, chunk, axis=1)
    mixed = join(lax.all_to_all(total(parts, own_residual), "tp", 0, 0))

    adopted = place(index, N_ROUNDS, arrived, adopt)
    adopted = place(index, 2 * N_ROUNDS, passed, adopt, adopted)
    return (mixed, adopted[None, None])


def solution(mesh):
    in_specs = (
        P("inst", "tp", None, None, None),
        P("inst", "tp", None, None, None, None),
        P("inst", None, None, None),
        P("inst", None, "tp"),
        P("inst", None, None),
        P("inst", None),
        P("tp", None),
    )
    out_specs = (P("inst", None, None), P("inst", "tp", None, None, None, None))
    return jax.shard_map(
        on_device, mesh=mesh, in_specs=in_specs, out_specs=out_specs, check_vma=False
    )
```

```python
import functools
import math

import jax
import jax.numpy as jnp
import numpy as np
from jax import lax
from jax.experimental import pallas as pl
from jax.experimental.pallas import tpu as pltpu
from jax.sharding import PartitionSpec as P

HD = 128
KVH = 8
QH = 32
GROUP = QH // KVH
NZ = 8
PAD = 8
MIB = 1 << 20
NEAR = (1, 8, 9)
FAR = (2, 4, 6)
ROUNDS = ((0, 0), (-3, 0), (0, 1), (-3, 1), (2, 0), (-1, 1), (2, 1), (-1, 0))
N_ROUNDS = len(ROUNDS)
EARLY = 3
FIRST = 5
SMALL = 4

ANY = pl.BlockSpec(memory_space=pl.ANY)
VMEM = pl.BlockSpec(memory_space=pltpu.VMEM)
SMEM = pl.BlockSpec(memory_space=pltpu.SMEM)


def round_target(rank, step):
    shift, flip = ROUNDS[step]
    high, low = divmod(rank, NZ)
    sign = 1 if low % 2 == 0 else -1
    return (high + flip) % 2 * NZ + (low + sign * shift) % NZ


def partner(rank):
    return rank ^ 1


def tables(count, rows):
    mine = np.zeros((count, N_ROUNDS), np.int32)
    for rank in range(count):
        for step in range(N_ROUNDS):
            mine[round_target(rank, step), step] = rank
    theirs = mine[[partner(rank) for rank in range(count)]]
    late = np.broadcast_to(np.arange(count, rows, dtype=np.int32), (count, rows - count))
    order = np.concatenate([mine, theirs, late], axis=1)
    place = np.arange(rows)[None, :, None] == order[:, None, :]
    select = np.concatenate([mine, late], axis=1)[:, :, None] == np.arange(rows)[None, None, :]
    return np.concatenate([mine, theirs], axis=1), place, select


def run_copies(copies):
    for copy in copies:
        copy.start()
    for copy in copies:
        copy.wait()


def extract_kernel(meta_ref, cache_ref, *rest):
    outs, (held, in_sem, out_sem) = rest[:N_ROUNDS], rest[N_ROUNDS:]
    rank = meta_ref[0]
    high, low = rank // NZ, rank % NZ
    sign = 1 - 2 * (low % 2)
    loads, stores = [], []
    for step, (shift, flip) in enumerate(ROUNDS):
        target = (high + flip) % 2 * NZ + (low + NZ + sign * shift) % NZ
        columns = pl.ds(pl.multiple_of(target // 2 * HD, HD), HD)
        loads.append(
            pltpu.make_async_copy(cache_ref.at[:, :, columns], held.at[step], in_sem.at[step])
        )
        stores.append(pltpu.make_async_copy(held.at[step], outs[step], out_sem.at[step]))
    for load in loads:
        load.start()
    for load, store in zip(loads, stores):
        load.wait()
        store.start()
    for store in stores:
        store.wait()


def extract(meta, cache):
    block = (2, cache.shape[1], HD)
    return pl.pallas_call(
        extract_kernel,
        out_shape=[jax.ShapeDtypeStruct(block, cache.dtype)] * N_ROUNDS,
        in_specs=[SMEM, ANY],
        out_specs=[ANY] * N_ROUNDS,
        scratch_shapes=[
            pltpu.VMEM((N_ROUNDS,) + block, cache.dtype),
            pltpu.SemaphoreType.DMA((N_ROUNDS,)),
            pltpu.SemaphoreType.DMA((N_ROUNDS,)),
        ],
        compiler_params=pltpu.CompilerParams(vmem_limit_bytes=60 * MIB),
        name="extract",
    )(meta, cache)


def place_kernel(offset, count, has_base, index_ref, *rest):
    blocks = rest[:count]
    out_ref, sem = rest[-3 if has_base == 2 else -2], rest[-1]
    run_copies([
        pltpu.make_async_copy(blocks[i], out_ref.at[index_ref[offset + i]], sem.at[i])
        for i in range(count)
    ])


def place(index, offset, blocks, rows, base=None, ready=None, carry=None):
    count = len(blocks)
    out = [jax.ShapeDtypeStruct((rows,) + blocks[0].shape, blocks[0].dtype)]
    operands, aliases = [], {}
    if base is not None:
        aliases[1 + count] = 0
        operands.append(base)
    if ready is not None:
        operands.append(ready)
    if carry is not None:
        aliases[1 + count + len(operands)] = 1
        operands.append(carry)
        out.append(jax.ShapeDtypeStruct(carry.shape, carry.dtype))
    return pl.pallas_call(
        functools.partial(place_kernel, offset, count, len(out)),
        out_shape=out,
        in_specs=[SMEM] + [VMEM] * count + [ANY] * len(operands),
        out_specs=[ANY] * len(out),
        scratch_shapes=[pltpu.SemaphoreType.DMA((count,))],
        input_output_aliases=aliases,
        compiler_params=pltpu.CompilerParams(vmem_limit_bytes=16 * MIB),
        name="place",
    )(index, *blocks, *operands)


def attend_kernel(first, heads, scale, len_ref, rows_ref, *rest):
    n_out = heads // 2
    blocks, outs = rest[: -5 - n_out], rest[-5 - n_out : -5]
    q_ref, k_ref, v_ref, prob_ref, blend_ref = rest[-5:]
    count = q_ref.shape[0] // PAD

    def block(b, kind):
        return blocks[0][b, kind] if len(blocks) == 1 else blocks[b][kind]

    new = GROUP * HD
    picked = slice(first, first + count)
    for g in range(PAD):
        spread = pl.ds(g, count, stride=PAD)
        lane = min(g, heads - 1) * HD
        q_ref[spread, :] = rows_ref[picked, lane : lane + HD]
        k_ref[spread, :] = rows_ref[picked, new : new + HD]
        v_ref[spread, :] = rows_ref[picked, new + HD : new + 2 * HD]
    for b in range(count):
        rows = slice(b * PAD, (b + 1) * PAD)
        scores = lax.dot_general(
            q_ref[rows, :].astype(jnp.bfloat16),
            block(b, 0),
            (((1,), (1,)), ((), ())),
            preferred_element_type=jnp.float32,
        )
        live = lax.broadcasted_iota(jnp.int32, scores.shape, 1) < len_ref[b]
        prob_ref[rows, :] = jnp.where(live, scores * scale, -1e30)
    scores = prob_ref[...]
    own = jnp.sum(q_ref[...] * k_ref[...], axis=-1, keepdims=True) * scale
    top = jnp.maximum(jnp.max(scores, axis=-1, keepdims=True), own)
    weights = jnp.exp(scores - top)
    own_weight = jnp.exp(own - top)
    total = jnp.sum(weights, axis=-1, keepdims=True) + own_weight
    prob_ref[...] = weights / total
    own_prob = (own_weight / total).astype(jnp.bfloat16).astype(jnp.float32)
    fresh = own_prob * v_ref[...]
    for b in range(count):
        rows = slice(b * PAD, (b + 1) * PAD)
        blended = jnp.dot(
            prob_ref[rows, :].astype(jnp.bfloat16),
            block(b, 1),
            preferred_element_type=jnp.float32,
        )
        blend_ref[rows, :] = blended + fresh[rows, :]
    for g in range(heads):
        outs[g // 2][:, g % 2 * HD : (g % 2 + 1) * HD] = blend_ref[pl.ds(g, count, stride=PAD), :]


def attend(first, heads, lengths, table, blocks):
    span = blocks[0].shape[-2]
    count = lengths.shape[0]
    wide = pltpu.VMEM((count * PAD, HD), jnp.float32)
    return pl.pallas_call(
        functools.partial(attend_kernel, first, heads, 1.0 / math.sqrt(HD)),
        out_shape=[jax.ShapeDtypeStruct((count, 2 * HD), jnp.float32)] * (heads // 2),
        in_specs=[SMEM] + [VMEM] * (1 + len(blocks)),
        out_specs=[VMEM] * (heads // 2),
        scratch_shapes=[wide, wide, wide, pltpu.VMEM((count * PAD, span), jnp.float32), wide],
        compiler_params=pltpu.CompilerParams(vmem_limit_bytes=16 * MIB),
        name="attend",
    )(lengths, table, *blocks)


def owner(rank, far, near):
    return ((rank ^ near) & 9) | (far << 1)


def project_kernel(meta_ref, place_ref, kept_ref, traded_ref, res_ref, weight_ref, *outs):
    gathered = jnp.concatenate([kept_ref[...], traded_ref[...], res_ref[...]], axis=0)
    attn = jnp.dot(
        place_ref[...], gathered.astype(jnp.bfloat16), preferred_element_type=jnp.float32
    ).astype(jnp.bfloat16)
    rank = meta_ref[0]
    for near, out_ref in zip((0,) + NEAR, outs):
        for far in range(4):
            chunk = out_ref.shape[2]
            columns = pl.ds(pl.multiple_of(owner(rank, far, near) * chunk, chunk), chunk)
            out_ref[far] = jnp.dot(
                attn, weight_ref[:, columns], preferred_element_type=jnp.float32
            ).astype(out_ref.dtype)


def project(meta, order, kept, traded, res, weight, count):
    shape = (4, order.shape[0], weight.shape[1] // count)
    return pl.pallas_call(
        project_kernel,
        out_shape=[jax.ShapeDtypeStruct(shape, jnp.bfloat16)] * 4,
        in_specs=[SMEM] + [VMEM] * 5,
        out_specs=[VMEM] * 4,
        compiler_params=pltpu.CompilerParams(vmem_limit_bytes=24 * MIB),
        name="project",
    )(meta, order, kept, traded, res, weight)


def near_kernel(meta_ref, *refs):
    parts, outs = refs[:4], refs[4:]
    mine = meta_ref[0] // 2 % 4
    for step, out_ref in enumerate(outs):
        far = mine ^ step
        summed = parts[0][far].astype(jnp.float32)
        for part in parts[1:]:
            summed = summed + part[far].astype(jnp.float32)
        out_ref[...] = summed


def near_sum(meta, parts):
    return pl.pallas_call(
        near_kernel,
        out_shape=[jax.ShapeDtypeStruct(parts[0].shape[1:], jnp.float32)] * 4,
        in_specs=[SMEM] + [VMEM] * 4,
        out_specs=[VMEM] * 4,
        compiler_params=pltpu.CompilerParams(vmem_limit_bytes=16 * MIB),
        name="near_sum",
    )(meta, *parts)


def far_kernel(*refs):
    parts, residual_ref, out_ref = refs[:4], refs[4], refs[5]
    summed = (parts[0][...] + parts[1][...]) + (parts[2][...] + parts[3][...])
    out_ref[...] = (residual_ref[...].astype(jnp.float32) + summed).astype(out_ref.dtype)


def far_sum(parts, residual):
    return pl.pallas_call(
        far_kernel,
        out_shape=jax.ShapeDtypeStruct(residual.shape, residual.dtype),
        in_specs=[VMEM] * 5,
        out_specs=VMEM,
        compiler_params=pltpu.CompilerParams(vmem_limit_bytes=16 * MIB),
        name="far_sum",
    )(*parts, residual)


def stack_kernel(meta_ref, *refs):
    parts, out_ref = refs[:4], refs[4]
    for step, part in enumerate(parts):
        out_ref[meta_ref[0] // 2 % 4 ^ step] = part[...]


def stack(meta, parts):
    return pl.pallas_call(
        stack_kernel,
        out_shape=jax.ShapeDtypeStruct((4,) + parts[0].shape, parts[0].dtype),
        in_specs=[SMEM] + [VMEM] * 4,
        out_specs=VMEM,
        compiler_params=pltpu.CompilerParams(vmem_limit_bytes=16 * MIB),
        name="stack",
    )(meta, *parts)


def join_kernel(meta_ref, *refs):
    parts, out_ref = refs[:4], refs[4]
    rank = meta_ref[0]
    for near, part in zip((0,) + NEAR, parts):
        chunk = part.shape[2]
        for far in range(4):
            columns = pl.ds(pl.multiple_of(owner(rank, far, near) * chunk, chunk), chunk)
            out_ref[0, :, columns] = part[far]


def join(meta, parts, count):
    _, rows, chunk = parts[0].shape
    return pl.pallas_call(
        join_kernel,
        out_shape=jax.ShapeDtypeStruct((1, rows, count * chunk), parts[0].dtype),
        in_specs=[SMEM] + [VMEM] * 4,
        out_specs=VMEM,
        compiler_params=pltpu.CompilerParams(vmem_limit_bytes=16 * MIB),
        name="join",
    )(meta, *parts)


def hop(value, inst_count, tp_count, target):
    half = inst_count // 2
    pairs = [
        (i * tp_count + t, (i + half) % inst_count * tp_count + target(t))
        for i in range(inst_count)
        for t in range(tp_count)
    ]
    return lax.ppermute(value, ("inst", "tp"), pairs)


def after(value, others):
    return lax.optimization_barrier((value, *others))[0] if others else value


def swap(value, tp_count, bits=1):
    return lax.ppermute(value, "tp", [(t, t ^ bits) for t in range(tp_count)])


def on_device(source_cache, resident_cache, new_kv, queries, residual, lengths, out_weight):
    tp_count = lax.axis_size("tp")
    inst_count = lax.axis_size("inst")
    rank = lax.axis_index("tp")
    rows = queries.shape[1]
    adopt = tp_count
    chunk = out_weight.shape[1] // tp_count
    meta = rank.reshape(1).astype(jnp.int32)

    handed = hop(lengths[0], inst_count, tp_count, lambda t: t)
    other_q = swap(queries[0], tp_count)
    sent = list(extract(after(meta, [handed, other_q]), source_cache[0, 0]))

    def send(step, block):
        return hop(block, inst_count, tp_count, lambda t: round_target(t, step))

    arrived = []
    for step in range(N_ROUNDS):
        arrived.append(send(step, sent[step]))
    passed = [swap(arrived[k], tp_count) for k in range(EARLY)]

    index, order, select = tables(tp_count, rows)
    index = lax.dynamic_index_in_dim(jnp.asarray(index), rank, keepdims=False)
    order = lax.dynamic_index_in_dim(jnp.asarray(order, jnp.bfloat16), rank, keepdims=False)
    select = lax.dynamic_index_in_dim(jnp.asarray(select, jnp.bfloat16), rank, keepdims=False)
    mine = index[:N_ROUNDS]
    fresh = lax.dynamic_slice_in_dim(new_kv[0], rank // 2 * HD, HD, axis=2)
    table = jnp.concatenate([queries[0], other_q, fresh.reshape(rows, 2 * HD)], axis=1)
    table = jnp.dot(select, table, preferred_element_type=jnp.float32)
    hit = mine[:, None] == jnp.arange(rows, dtype=jnp.int32)[None, :]
    adopt_len = jnp.sum(jnp.where(hit, handed[None, :], 0), axis=1)
    (res,) = attend(N_ROUNDS, 2, lengths[0, adopt:], table, [resident_cache[0, 0]])
    own_residual = lax.dynamic_slice_in_dim(residual[0], rank * chunk, chunk, axis=1)

    table = after(table, [*passed, res, own_residual])
    kept, traded = attend(0, GROUP, adopt_len, table, arrived)

    adopted, done = None, 0
    def beside(ready, count):
        nonlocal adopted, done
        blocks = (arrived + passed)[done : done + count]
        carry = arrived[len(passed)]
        adopted, carry = place(index, done, blocks, adopt, adopted, ready, carry)
        done += count
        passed.append(swap(carry, tp_count))

    traded = swap(traded, tp_count)
    beside(kept, 2)
    parts = project(meta, order, kept, traded, res, out_weight, tp_count)
    first = parts[0]
    parts = [first] + [swap(part, tp_count, bits) for part, bits in zip(parts[1:], NEAR)]
    beside(first, 3)
    parts = near_sum(meta, [after(parts[0], passed[:-1])] + parts[1:])
    first = parts[0]
    parts = [first] + [swap(part, tp_count, bits) for part, bits in zip(parts[1:], FAR)]
    beside(first, 3)
    mixed = far_sum([after(parts[0], passed[:-1])] + parts[1:], own_residual)
    parts = [mixed] + [swap(mixed, tp_count, bits) for bits in FAR]
    beside(mixed, 3)
    mixed = stack(meta, [after(mixed, passed[:-1])] + parts[1:])
    parts = [mixed] + [swap(mixed, tp_count, bits) for bits in NEAR]
    beside(mixed, 3)
    mixed = join(meta, parts, tp_count)
    (adopted,) = place(index, done, (arrived + passed)[done:], adopt, adopted)
    return (mixed, adopted[None, None])


def solution(mesh):
    in_specs = (
        P("inst", "tp", None, None, None),
        P("inst", "tp", None, None, None, None),
        P("inst", None, None, None),
        P("inst", None, "tp"),
        P("inst", None, None),
        P("inst", None),
        P("tp", None),
    )
    out_specs = (P("inst", None, None), P("inst", "tp", None, None, None, None))
    return jax.shard_map(
        on_device, mesh=mesh, in_specs=in_specs, out_specs=out_specs, check_vma=False
    )
```

```python
import functools
import math

import jax
import jax.numpy as jnp
import numpy as np
from jax import lax
from jax.experimental import pallas as pl
from jax.experimental.pallas import tpu as pltpu
from jax.sharding import PartitionSpec as P

HD = 128
KVH = 8
QH = 32
GROUP = QH // KVH
NZ = 8
PAD = 8
MIB = 1 << 20
NEAR = (1, 8, 9)
FAR = (2, 4, 6)
ROUNDS = ((0, 0), (-3, 0), (0, 1), (-3, 1), (2, 0), (-1, 1), (2, 1), (-1, 0))
N_ROUNDS = len(ROUNDS)
PLACED = 13
EARLY = 5
NEXT = 2
LAST = 1
FIRST = 0
SMALL = -1

ANY = pl.BlockSpec(memory_space=pl.ANY)
VMEM = pl.BlockSpec(memory_space=pltpu.VMEM)
SMEM = pl.BlockSpec(memory_space=pltpu.SMEM)


def round_target(rank, step):
    shift, flip = ROUNDS[step]
    high, low = divmod(rank, NZ)
    sign = 1 if low % 2 == 0 else -1
    return (high + flip) % 2 * NZ + (low + sign * shift) % NZ


def partner(rank):
    return rank ^ 1


def tables(count, rows):
    mine = np.zeros((count, N_ROUNDS), np.int32)
    for rank in range(count):
        for step in range(N_ROUNDS):
            mine[round_target(rank, step), step] = rank
    theirs = mine[[partner(rank) for rank in range(count)]]
    late = np.broadcast_to(np.arange(count, rows, dtype=np.int32), (count, rows - count))
    order = np.concatenate([mine, theirs, late], axis=1)
    place = np.arange(rows)[None, :, None] == order[:, None, :]
    select = np.concatenate([mine, late], axis=1)[:, :, None] == np.arange(rows)[None, None, :]
    return np.concatenate([mine, theirs], axis=1), place, select


def run_copies(copies):
    for copy in copies:
        copy.start()
    for copy in copies:
        copy.wait()


def extract_kernel(meta_ref, cache_ref, *rest):
    outs, (held, in_sem, out_sem) = rest[:N_ROUNDS], rest[N_ROUNDS:]
    rank = meta_ref[0]
    high, low = rank // NZ, rank % NZ
    sign = 1 - 2 * (low % 2)
    loads, stores = [], []
    for step, (shift, flip) in enumerate(ROUNDS):
        target = (high + flip) % 2 * NZ + (low + NZ + sign * shift) % NZ
        columns = pl.ds(pl.multiple_of(target // 2 * HD, HD), HD)
        loads.append(
            pltpu.make_async_copy(cache_ref.at[:, :, columns], held.at[step], in_sem.at[step])
        )
        stores.append(pltpu.make_async_copy(held.at[step], outs[step], out_sem.at[step]))
    for load in loads:
        load.start()
    for load, store in zip(loads, stores):
        load.wait()
        store.start()
    for store in stores:
        store.wait()


def extract(meta, cache):
    block = (2, cache.shape[1], HD)
    return pl.pallas_call(
        extract_kernel,
        out_shape=[jax.ShapeDtypeStruct(block, cache.dtype)] * N_ROUNDS,
        in_specs=[SMEM, ANY],
        out_specs=[ANY] * N_ROUNDS,
        scratch_shapes=[
            pltpu.VMEM((N_ROUNDS,) + block, cache.dtype),
            pltpu.SemaphoreType.DMA((N_ROUNDS,)),
            pltpu.SemaphoreType.DMA((N_ROUNDS,)),
        ],
        compiler_params=pltpu.CompilerParams(vmem_limit_bytes=60 * MIB),
        name="extract",
    )(meta, cache)


def place_kernel(offset, count, n_out, index_ref, *rest):
    blocks, out_ref, sem = rest[:count], rest[-1 - n_out], rest[-1]
    run_copies([
        pltpu.make_async_copy(blocks[i], out_ref.at[index_ref[offset + i]], sem.at[i])
        for i in range(count)
    ])


def place(index, offset, blocks, rows, base=None, ready=None, carry=()):
    count = len(blocks)
    out = [jax.ShapeDtypeStruct((rows,) + blocks[0].shape, blocks[0].dtype)]
    operands, aliases = [], {}
    if base is not None:
        aliases[1 + count] = 0
        operands.append(base)
    if ready is not None:
        operands.append(ready)
    for array in carry:
        aliases[1 + count + len(operands)] = len(out)
        operands.append(array)
        out.append(jax.ShapeDtypeStruct(array.shape, array.dtype))
    return pl.pallas_call(
        functools.partial(place_kernel, offset, count, len(out)),
        out_shape=out,
        in_specs=[SMEM] + [VMEM] * count + [ANY] * len(operands),
        out_specs=[ANY] * len(out),
        scratch_shapes=[pltpu.SemaphoreType.DMA((count,))],
        input_output_aliases=aliases,
        compiler_params=pltpu.CompilerParams(vmem_limit_bytes=16 * MIB),
        name="place",
    )(index, *blocks, *operands)


def attend_kernel(first, heads, scale, len_ref, rows_ref, *rest):
    n_out = heads // 2
    blocks, outs = rest[: -5 - n_out], rest[-5 - n_out : -5]
    q_ref, k_ref, v_ref, prob_ref, blend_ref = rest[-5:]
    count = q_ref.shape[0] // PAD

    def block(b, kind):
        return blocks[0][b, kind] if len(blocks) == 1 else blocks[b][kind]

    new = GROUP * HD
    picked = slice(first, first + count)
    for g in range(PAD):
        spread = pl.ds(g, count, stride=PAD)
        lane = min(g, heads - 1) * HD
        q_ref[spread, :] = rows_ref[picked, lane : lane + HD]
        k_ref[spread, :] = rows_ref[picked, new : new + HD]
        v_ref[spread, :] = rows_ref[picked, new + HD : new + 2 * HD]
    for b in range(count):
        rows = slice(b * PAD, (b + 1) * PAD)
        scores = lax.dot_general(
            q_ref[rows, :].astype(jnp.bfloat16),
            block(b, 0),
            (((1,), (1,)), ((), ())),
            preferred_element_type=jnp.float32,
        )
        live = lax.broadcasted_iota(jnp.int32, scores.shape, 1) < len_ref[b]
        prob_ref[rows, :] = jnp.where(live, scores * scale, -1e30)
    scores = prob_ref[...]
    own = jnp.sum(q_ref[...] * k_ref[...], axis=-1, keepdims=True) * scale
    top = jnp.maximum(jnp.max(scores, axis=-1, keepdims=True), own)
    weights = jnp.exp(scores - top)
    own_weight = jnp.exp(own - top)
    total = jnp.sum(weights, axis=-1, keepdims=True) + own_weight
    prob_ref[...] = weights / total
    own_prob = (own_weight / total).astype(jnp.bfloat16).astype(jnp.float32)
    fresh = own_prob * v_ref[...]
    for b in range(count):
        rows = slice(b * PAD, (b + 1) * PAD)
        blended = jnp.dot(
            prob_ref[rows, :].astype(jnp.bfloat16),
            block(b, 1),
            preferred_element_type=jnp.float32,
        )
        blend_ref[rows, :] = blended + fresh[rows, :]
    for g in range(heads):
        outs[g // 2][:, g % 2 * HD : (g % 2 + 1) * HD] = blend_ref[pl.ds(g, count, stride=PAD), :]


def attend(first, heads, lengths, table, blocks):
    span = blocks[0].shape[-2]
    count = lengths.shape[0]
    wide = pltpu.VMEM((count * PAD, HD), jnp.float32)
    return pl.pallas_call(
        functools.partial(attend_kernel, first, heads, 1.0 / math.sqrt(HD)),
        out_shape=[jax.ShapeDtypeStruct((count, 2 * HD), jnp.float32)] * (heads // 2),
        in_specs=[SMEM] + [VMEM] * (1 + len(blocks)),
        out_specs=[VMEM] * (heads // 2),
        scratch_shapes=[wide, wide, wide, pltpu.VMEM((count * PAD, span), jnp.float32), wide],
        compiler_params=pltpu.CompilerParams(vmem_limit_bytes=16 * MIB),
        name="attend",
    )(lengths, table, *blocks)


def owner(rank, far, near):
    return ((rank ^ near) & 9) | (far << 1)


def project_kernel(meta_ref, place_ref, kept_ref, traded_ref, res_ref, weight_ref, *outs):
    gathered = jnp.concatenate([kept_ref[...], traded_ref[...], res_ref[...]], axis=0)
    attn = jnp.dot(
        place_ref[...], gathered.astype(jnp.bfloat16), preferred_element_type=jnp.float32
    ).astype(jnp.bfloat16)
    rank = meta_ref[0]
    for near, out_ref in zip((0,) + NEAR, outs):
        for far in range(4):
            chunk = out_ref.shape[2]
            columns = pl.ds(pl.multiple_of(owner(rank, far, near) * chunk, chunk), chunk)
            out_ref[far] = jnp.dot(
                attn, weight_ref[:, columns], preferred_element_type=jnp.float32
            ).astype(out_ref.dtype)


def project(meta, order, kept, traded, res, weight, count):
    shape = (4, order.shape[0], weight.shape[1] // count)
    return pl.pallas_call(
        project_kernel,
        out_shape=[jax.ShapeDtypeStruct(shape, jnp.bfloat16)] * 4,
        in_specs=[SMEM] + [VMEM] * 5,
        out_specs=[VMEM] * 4,
        compiler_params=pltpu.CompilerParams(vmem_limit_bytes=24 * MIB),
        name="project",
    )(meta, order, kept, traded, res, weight)


def near_kernel(*refs):
    parts, out_ref = refs[:4], refs[4]
    for far in range(4):
        summed = parts[0][far].astype(jnp.float32)
        for part in parts[1:]:
            summed = summed + part[far].astype(jnp.float32)
        out_ref[far] = summed.astype(out_ref.dtype)


def near_sum(parts):
    return pl.pallas_call(
        near_kernel,
        out_shape=jax.ShapeDtypeStruct(parts[0].shape, parts[0].dtype),
        in_specs=[VMEM] * 4,
        out_specs=VMEM,
        compiler_params=pltpu.CompilerParams(vmem_limit_bytes=16 * MIB),
        name="near_sum",
    )(*parts)


def far_kernel(meta_ref, *refs):
    parts, residual_ref, out_ref = refs[:4], refs[4], refs[5]
    chunk = out_ref.shape[2]
    for far in range(4):
        one, two, three, four = [part[far].astype(jnp.float32) for part in parts]
        summed = (one + two) + (three + four)
        columns = pl.ds(pl.multiple_of(owner(meta_ref[0], far, 0) * chunk, chunk), chunk)
        own = residual_ref[:, columns].astype(jnp.float32)
        out_ref[far] = (own + summed).astype(out_ref.dtype)


def far_sum(meta, parts, residual):
    return pl.pallas_call(
        far_kernel,
        out_shape=jax.ShapeDtypeStruct(parts[0].shape, residual.dtype),
        in_specs=[SMEM] + [VMEM] * 5,
        out_specs=VMEM,
        compiler_params=pltpu.CompilerParams(vmem_limit_bytes=16 * MIB),
        name="far_sum",
    )(meta, *parts, residual)


def join_kernel(meta_ref, *refs):
    parts, out_ref = refs[:4], refs[4]
    rank = meta_ref[0]
    for near, part in zip((0,) + NEAR, parts):
        chunk = part.shape[2]
        for far in range(4):
            columns = pl.ds(pl.multiple_of(owner(rank, far, near) * chunk, chunk), chunk)
            out_ref[0, :, columns] = part[far]


def join(meta, parts, count):
    _, rows, chunk = parts[0].shape
    return pl.pallas_call(
        join_kernel,
        out_shape=jax.ShapeDtypeStruct((1, rows, count * chunk), parts[0].dtype),
        in_specs=[SMEM] + [VMEM] * 4,
        out_specs=VMEM,
        compiler_params=pltpu.CompilerParams(vmem_limit_bytes=16 * MIB),
        name="join",
    )(meta, *parts)


def hop(value, inst_count, tp_count, target):
    half = inst_count // 2
    pairs = [
        (i * tp_count + t, (i + half) % inst_count * tp_count + target(t))
        for i in range(inst_count)
        for t in range(tp_count)
    ]
    return lax.ppermute(value, ("inst", "tp"), pairs)


def after(value, others):
    return lax.optimization_barrier((value, *others))[0] if others else value


def swap(value, tp_count, bits=1):
    return lax.ppermute(value, "tp", [(t, t ^ bits) for t in range(tp_count)])


def on_device(source_cache, resident_cache, new_kv, queries, residual, lengths, out_weight):
    tp_count = lax.axis_size("tp")
    inst_count = lax.axis_size("inst")
    rank = lax.axis_index("tp")
    rows = queries.shape[1]
    adopt = tp_count
    chunk = out_weight.shape[1] // tp_count
    meta = rank.reshape(1).astype(jnp.int32)


    def send(step, block):
        return hop(block, inst_count, tp_count, lambda t: round_target(t, step))

    handed = hop(lengths[0], inst_count, tp_count, lambda t: t)
    other_q = swap(queries[0], tp_count)
    sent = list(extract(after(meta, [handed, other_q]), source_cache[0, 0]))
    arrived = [send(step, sent[step]) for step in range(N_ROUNDS)]

    index, order, select = tables(tp_count, rows)
    index = lax.dynamic_index_in_dim(jnp.asarray(index), rank, keepdims=False)
    order = lax.dynamic_index_in_dim(jnp.asarray(order, jnp.bfloat16), rank, keepdims=False)
    select = lax.dynamic_index_in_dim(jnp.asarray(select, jnp.bfloat16), rank, keepdims=False)
    mine = index[:N_ROUNDS]
    fresh = lax.dynamic_slice_in_dim(new_kv[0], rank // 2 * HD, HD, axis=2)
    table = jnp.concatenate([queries[0], other_q, fresh.reshape(rows, 2 * HD)], axis=1)
    table = jnp.dot(select, table, preferred_element_type=jnp.float32)
    hit = mine[:, None] == jnp.arange(rows, dtype=jnp.int32)[None, :]
    adopt_len = jnp.sum(jnp.where(hit, handed[None, :], 0), axis=1)
    (res,) = attend(N_ROUNDS, 2, lengths[0, adopt:], table, [resident_cache[0, 0]])

    passed = [swap(block, tp_count) for block in arrived[:EARLY]]
    table = after(table, [*passed, res])
    kept, traded = attend(0, GROUP, adopt_len, table, arrived)

    def pass_on(ready, count):
        for _ in range(count):
            block = after(arrived[len(passed)], [ready])
            passed.append(swap(block, tp_count))

    traded = swap(traded, tp_count)
    parts = project(meta, order, kept, traded, res, out_weight, tp_count)
    pass_on(parts[0], 1)
    parts = [parts[0]] + [swap(part, tp_count, bits) for part, bits in zip(parts[1:], NEAR)]
    part = near_sum([after(parts[0], passed[:-1])] + parts[1:])
    pass_on(part, 1)
    parts = [part] + [swap(part, tp_count, bits) for bits in FAR]
    mixed = far_sum(meta, [after(part, passed[:-1])] + parts[1:], residual[0])
    pass_on(mixed, 1)
    parts = [mixed] + [swap(mixed, tp_count, bits) for bits in NEAR]
    (adopted,) = place(index, 0, (arrived + passed)[:PLACED], adopt, None, mixed)
    mixed = join(meta, parts, tp_count)
    (adopted,) = place(index, PLACED, (arrived + passed)[PLACED:], adopt, adopted)
    return (mixed, adopted[None, None])


def solution(mesh):
    in_specs = (
        P("inst", "tp", None, None, None),
        P("inst", "tp", None, None, None, None),
        P("inst", None, None, None),
        P("inst", None, "tp"),
        P("inst", None, None),
        P("inst", None),
        P("tp", None),
    )
    out_specs = (P("inst", None, None), P("inst", "tp", None, None, None, None))
    return jax.shard_map(
        on_device, mesh=mesh, in_specs=in_specs, out_specs=out_specs, check_vma=False
    )
```

```python
import functools
import math

import jax
import jax.numpy as jnp
import numpy as np
from jax import lax
from jax.experimental import pallas as pl
from jax.experimental.pallas import tpu as pltpu
from jax.sharding import PartitionSpec as P

HD = 128
KVH = 8
QH = 32
GROUP = QH // KVH
NZ = 8
PAD = 8
MIB = 1 << 20
NEAR = (1, 8, 9)
FAR = (2, 4, 6)
ROUNDS = ((0, 0), (-3, 0), (0, 1), (-3, 1), (2, 0), (-1, 1), (2, 1), (-1, 0))
N_ROUNDS = len(ROUNDS)
PLACED = 13
EARLY = 5

ANY = pl.BlockSpec(memory_space=pl.ANY)
VMEM = pl.BlockSpec(memory_space=pltpu.VMEM)
SMEM = pl.BlockSpec(memory_space=pltpu.SMEM)


def round_target(rank, step):
    shift, flip = ROUNDS[step]
    high, low = divmod(rank, NZ)
    sign = 1 if low % 2 == 0 else -1
    return (high + flip) % 2 * NZ + (low + sign * shift) % NZ


def partner(rank):
    return rank ^ 1


def tables(count, rows):
    mine = np.zeros((count, N_ROUNDS), np.int32)
    for rank in range(count):
        for step in range(N_ROUNDS):
            mine[round_target(rank, step), step] = rank
    theirs = mine[[partner(rank) for rank in range(count)]]
    late = np.broadcast_to(np.arange(count, rows, dtype=np.int32), (count, rows - count))
    order = np.concatenate([mine, theirs, late], axis=1)
    place = np.arange(rows)[None, :, None] == order[:, None, :]
    select = np.concatenate([mine, late], axis=1)[:, :, None] == np.arange(rows)[None, None, :]
    return np.concatenate([mine, theirs], axis=1), place, select


def run_copies(copies):
    for copy in copies:
        copy.start()
    for copy in copies:
        copy.wait()


def extract_kernel(steps, meta_ref, cache_ref, *rest):
    outs, (held, in_sem, out_sem) = rest[: len(steps)], rest[len(steps) :]
    rank = meta_ref[0]
    high, low = rank // NZ, rank % NZ
    sign = 1 - 2 * (low % 2)
    loads, stores = [], []
    for step, (shift, flip) in enumerate([ROUNDS[step] for step in steps]):
        target = (high + flip) % 2 * NZ + (low + NZ + sign * shift) % NZ
        columns = pl.ds(pl.multiple_of(target // 2 * HD, HD), HD)
        loads.append(
            pltpu.make_async_copy(cache_ref.at[:, :, columns], held.at[step], in_sem.at[step])
        )
        stores.append(pltpu.make_async_copy(held.at[step], outs[step], out_sem.at[step]))
    for load in loads:
        load.start()
    for load, store in zip(loads, stores):
        load.wait()
        store.start()
    for store in stores:
        store.wait()


def extract(steps, meta, cache):
    block = (2, cache.shape[1], HD)
    return pl.pallas_call(
        functools.partial(extract_kernel, steps),
        out_shape=[jax.ShapeDtypeStruct(block, cache.dtype)] * len(steps),
        in_specs=[SMEM, ANY],
        out_specs=[ANY] * len(steps),
        scratch_shapes=[
            pltpu.VMEM((len(steps),) + block, cache.dtype),
            pltpu.SemaphoreType.DMA((len(steps),)),
            pltpu.SemaphoreType.DMA((len(steps),)),
        ],
        compiler_params=pltpu.CompilerParams(vmem_limit_bytes=60 * MIB),
        name="extract",
    )(meta, cache)


def place_kernel(offset, count, n_out, index_ref, *rest):
    blocks, out_ref, sem = rest[:count], rest[-1 - n_out], rest[-1]
    run_copies([
        pltpu.make_async_copy(blocks[i], out_ref.at[index_ref[offset + i]], sem.at[i])
        for i in range(count)
    ])


def place(index, offset, blocks, rows, base=None, ready=None, carry=()):
    count = len(blocks)
    out = [jax.ShapeDtypeStruct((rows,) + blocks[0].shape, blocks[0].dtype)]
    operands, aliases = [], {}
    if base is not None:
        aliases[1 + count] = 0
        operands.append(base)
    if ready is not None:
        operands.append(ready)
    for array in carry:
        aliases[1 + count + len(operands)] = len(out)
        operands.append(array)
        out.append(jax.ShapeDtypeStruct(array.shape, array.dtype))
    return pl.pallas_call(
        functools.partial(place_kernel, offset, count, len(out)),
        out_shape=out,
        in_specs=[SMEM] + [VMEM] * count + [ANY] * len(operands),
        out_specs=[ANY] * len(out),
        scratch_shapes=[pltpu.SemaphoreType.DMA((count,))],
        input_output_aliases=aliases,
        compiler_params=pltpu.CompilerParams(vmem_limit_bytes=16 * MIB),
        name="place",
    )(index, *blocks, *operands)


def attend_kernel(first, heads, scale, len_ref, rows_ref, *rest):
    n_out = heads // 2
    blocks, outs = rest[: -5 - n_out], rest[-5 - n_out : -5]
    q_ref, k_ref, v_ref, prob_ref, blend_ref = rest[-5:]
    count = q_ref.shape[0] // PAD

    def block(b, kind):
        return blocks[0][b, kind] if len(blocks) == 1 else blocks[b][kind]

    new = GROUP * HD
    picked = slice(first, first + count)
    for g in range(PAD):
        spread = pl.ds(g, count, stride=PAD)
        lane = min(g, heads - 1) * HD
        q_ref[spread, :] = rows_ref[picked, lane : lane + HD]
        k_ref[spread, :] = rows_ref[picked, new : new + HD]
        v_ref[spread, :] = rows_ref[picked, new + HD : new + 2 * HD]
    for b in range(count):
        rows = slice(b * PAD, (b + 1) * PAD)
        scores = lax.dot_general(
            q_ref[rows, :].astype(jnp.bfloat16),
            block(b, 0),
            (((1,), (1,)), ((), ())),
            preferred_element_type=jnp.float32,
        )
        live = lax.broadcasted_iota(jnp.int32, scores.shape, 1) < len_ref[b]
        prob_ref[rows, :] = jnp.where(live, scores * scale, -1e30)
    scores = prob_ref[...]
    own = jnp.sum(q_ref[...] * k_ref[...], axis=-1, keepdims=True) * scale
    top = jnp.maximum(jnp.max(scores, axis=-1, keepdims=True), own)
    weights = jnp.exp(scores - top)
    own_weight = jnp.exp(own - top)
    total = jnp.sum(weights, axis=-1, keepdims=True) + own_weight
    prob_ref[...] = weights / total
    own_prob = (own_weight / total).astype(jnp.bfloat16).astype(jnp.float32)
    fresh = own_prob * v_ref[...]
    for b in range(count):
        rows = slice(b * PAD, (b + 1) * PAD)
        blended = jnp.dot(
            prob_ref[rows, :].astype(jnp.bfloat16),
            block(b, 1),
            preferred_element_type=jnp.float32,
        )
        blend_ref[rows, :] = blended + fresh[rows, :]
    for g in range(heads):
        outs[g // 2][:, g % 2 * HD : (g % 2 + 1) * HD] = blend_ref[pl.ds(g, count, stride=PAD), :]


def attend(first, heads, lengths, table, blocks):
    span = blocks[0].shape[-2]
    count = lengths.shape[0]
    wide = pltpu.VMEM((count * PAD, HD), jnp.float32)
    return pl.pallas_call(
        functools.partial(attend_kernel, first, heads, 1.0 / math.sqrt(HD)),
        out_shape=[jax.ShapeDtypeStruct((count, 2 * HD), jnp.float32)] * (heads // 2),
        in_specs=[SMEM] + [VMEM] * (1 + len(blocks)),
        out_specs=[VMEM] * (heads // 2),
        scratch_shapes=[wide, wide, wide, pltpu.VMEM((count * PAD, span), jnp.float32), wide],
        compiler_params=pltpu.CompilerParams(vmem_limit_bytes=16 * MIB),
        name="attend",
    )(lengths, table, *blocks)


def owner(rank, far, near):
    return ((rank ^ near) & 9) | (far << 1)


def project_kernel(meta_ref, place_ref, kept_ref, traded_ref, res_ref, weight_ref, *outs):
    gathered = jnp.concatenate([kept_ref[...], traded_ref[...], res_ref[...]], axis=0)
    attn = jnp.dot(
        place_ref[...], gathered.astype(jnp.bfloat16), preferred_element_type=jnp.float32
    ).astype(jnp.bfloat16)
    rank = meta_ref[0]
    for near, out_ref in zip((0,) + NEAR, outs):
        for far in range(4):
            chunk = out_ref.shape[2]
            columns = pl.ds(pl.multiple_of(owner(rank, far, near) * chunk, chunk), chunk)
            out_ref[far] = jnp.dot(
                attn, weight_ref[:, columns], preferred_element_type=jnp.float32
            ).astype(out_ref.dtype)


def project(meta, order, kept, traded, res, weight, count):
    shape = (4, order.shape[0], weight.shape[1] // count)
    return pl.pallas_call(
        project_kernel,
        out_shape=[jax.ShapeDtypeStruct(shape, jnp.bfloat16)] * 4,
        in_specs=[SMEM] + [VMEM] * 5,
        out_specs=[VMEM] * 4,
        compiler_params=pltpu.CompilerParams(vmem_limit_bytes=24 * MIB),
        name="project",
    )(meta, order, kept, traded, res, weight)


def near_kernel(*refs):
    parts, out_ref = refs[:4], refs[4]
    for far in range(4):
        summed = parts[0][far].astype(jnp.float32)
        for part in parts[1:]:
            summed = summed + part[far].astype(jnp.float32)
        out_ref[far] = summed.astype(out_ref.dtype)


def near_sum(parts):
    return pl.pallas_call(
        near_kernel,
        out_shape=jax.ShapeDtypeStruct(parts[0].shape, parts[0].dtype),
        in_specs=[VMEM] * 4,
        out_specs=VMEM,
        compiler_params=pltpu.CompilerParams(vmem_limit_bytes=16 * MIB),
        name="near_sum",
    )(*parts)


def far_kernel(meta_ref, *refs):
    parts, residual_ref, out_ref = refs[:4], refs[4], refs[5]
    chunk = out_ref.shape[2]
    for far in range(4):
        one, two, three, four = [part[far].astype(jnp.float32) for part in parts]
        summed = (one + two) + (three + four)
        columns = pl.ds(pl.multiple_of(owner(meta_ref[0], far, 0) * chunk, chunk), chunk)
        own = residual_ref[:, columns].astype(jnp.float32)
        out_ref[far] = (own + summed).astype(out_ref.dtype)


def far_sum(meta, parts, residual):
    return pl.pallas_call(
        far_kernel,
        out_shape=jax.ShapeDtypeStruct(parts[0].shape, residual.dtype),
        in_specs=[SMEM] + [VMEM] * 5,
        out_specs=VMEM,
        compiler_params=pltpu.CompilerParams(vmem_limit_bytes=16 * MIB),
        name="far_sum",
    )(meta, *parts, residual)


def join_kernel(meta_ref, *refs):
    parts, out_ref = refs[:4], refs[4]
    rank = meta_ref[0]
    for near, part in zip((0,) + NEAR, parts):
        chunk = part.shape[2]
        for far in range(4):
            columns = pl.ds(pl.multiple_of(owner(rank, far, near) * chunk, chunk), chunk)
            out_ref[0, :, columns] = part[far]


def join(meta, parts, count):
    _, rows, chunk = parts[0].shape
    return pl.pallas_call(
        join_kernel,
        out_shape=jax.ShapeDtypeStruct((1, rows, count * chunk), parts[0].dtype),
        in_specs=[SMEM] + [VMEM] * 4,
        out_specs=VMEM,
        compiler_params=pltpu.CompilerParams(vmem_limit_bytes=16 * MIB),
        name="join",
    )(meta, *parts)


def hop(value, inst_count, tp_count, target):
    half = inst_count // 2
    pairs = [
        (i * tp_count + t, (i + half) % inst_count * tp_count + target(t))
        for i in range(inst_count)
        for t in range(tp_count)
    ]
    return lax.ppermute(value, ("inst", "tp"), pairs)


def after(value, others):
    return lax.optimization_barrier((value, *others))[0] if others else value


def swap(value, tp_count, bits=1):
    return lax.ppermute(value, "tp", [(t, t ^ bits) for t in range(tp_count)])


def on_device(source_cache, resident_cache, new_kv, queries, residual, lengths, out_weight):
    tp_count = lax.axis_size("tp")
    inst_count = lax.axis_size("inst")
    rank = lax.axis_index("tp")
    rows = queries.shape[1]
    adopt = tp_count
    chunk = out_weight.shape[1] // tp_count
    meta = rank.reshape(1).astype(jnp.int32)


    def send(step, block):
        return hop(block, inst_count, tp_count, lambda t: round_target(t, step))

    handed = hop(lengths[0], inst_count, tp_count, lambda t: t)
    other_q = swap(queries[0], tp_count)
    first = (4, 0)
    rest = tuple(step for step in range(N_ROUNDS) if step not in first)
    sent = dict(zip(first, extract(first, meta, source_cache[0, 0])))
    sent.update(zip(rest, extract(rest, meta, source_cache[0, 0])))
    sent = [
        sent[step] if step in first else after(sent[step], [handed, other_q])
        for step in range(N_ROUNDS)
    ]
    arrived = [send(step, sent[step]) for step in range(N_ROUNDS)]

    index, order, select = tables(tp_count, rows)
    index = lax.dynamic_index_in_dim(jnp.asarray(index), rank, keepdims=False)
    order = lax.dynamic_index_in_dim(jnp.asarray(order, jnp.bfloat16), rank, keepdims=False)
    select = lax.dynamic_index_in_dim(jnp.asarray(select, jnp.bfloat16), rank, keepdims=False)
    mine = index[:N_ROUNDS]
    fresh = lax.dynamic_slice_in_dim(new_kv[0], rank // 2 * HD, HD, axis=2)
    table = jnp.concatenate([queries[0], other_q, fresh.reshape(rows, 2 * HD)], axis=1)
    table = jnp.dot(select, table, preferred_element_type=jnp.float32)
    hit = mine[:, None] == jnp.arange(rows, dtype=jnp.int32)[None, :]
    adopt_len = jnp.sum(jnp.where(hit, handed[None, :], 0), axis=1)
    (res,) = attend(N_ROUNDS, 2, lengths[0, adopt:], table, [resident_cache[0, 0]])

    passed = [swap(block, tp_count) for block in arrived[:EARLY]]
    table = after(table, [*passed, res])
    kept, traded = attend(0, GROUP, adopt_len, table, arrived)

    def pass_on(ready, count):
        for _ in range(count):
            block = after(arrived[len(passed)], [ready])
            passed.append(swap(block, tp_count))

    traded = swap(traded, tp_count)
    parts = project(meta, order, kept, traded, res, out_weight, tp_count)
    pass_on(parts[0], 1)
    parts = [parts[0]] + [swap(part, tp_count, bits) for part, bits in zip(parts[1:], NEAR)]
    part = near_sum([after(parts[0], passed[:-1])] + parts[1:])
    pass_on(part, 1)
    parts = [part] + [swap(part, tp_count, bits) for bits in FAR]
    mixed = far_sum(meta, [after(part, passed[:-1])] + parts[1:], residual[0])
    pass_on(mixed, 1)
    parts = [mixed] + [swap(mixed, tp_count, bits) for bits in NEAR]
    (adopted,) = place(index, 0, (arrived + passed)[:PLACED], adopt, None, mixed)
    mixed = join(meta, parts, tp_count)
    (adopted,) = place(index, PLACED, (arrived + passed)[PLACED:], adopt, adopted)
    return (mixed, adopted[None, None])


def solution(mesh):
    in_specs = (
        P("inst", "tp", None, None, None),
        P("inst", "tp", None, None, None, None),
        P("inst", None, None, None),
        P("inst", None, "tp"),
        P("inst", None, None),
        P("inst", None),
        P("tp", None),
    )
    out_specs = (P("inst", None, None), P("inst", "tp", None, None, None, None))
    return jax.shard_map(
        on_device, mesh=mesh, in_specs=in_specs, out_specs=out_specs, check_vma=False
    )
```

```python
import functools
import math

import jax
import jax.numpy as jnp
import numpy as np
from jax import lax
from jax.experimental import pallas as pl
from jax.experimental.pallas import tpu as pltpu
from jax.sharding import PartitionSpec as P

HD = 128
KVH = 8
QH = 32
GROUP = QH // KVH
NZ = 8
PAD = 8
MIB = 1 << 20
NEAR = (1, 8, 9)
FAR = (2, 4, 6)
ROUNDS = ((0, 0), (-3, 0), (0, 1), (-3, 1), (2, 0), (-1, 1), (2, 1), (-1, 0))
N_ROUNDS = len(ROUNDS)
PLACED = 13
EARLY = 5

ANY = pl.BlockSpec(memory_space=pl.ANY)
VMEM = pl.BlockSpec(memory_space=pltpu.VMEM)
SMEM = pl.BlockSpec(memory_space=pltpu.SMEM)


def round_target(rank, step):
    shift, flip = ROUNDS[step]
    high, low = divmod(rank, NZ)
    sign = 1 if low % 2 == 0 else -1
    return (high + flip) % 2 * NZ + (low + sign * shift) % NZ


def partner(rank):
    return rank ^ 1


def tables(count, rows):
    mine = np.zeros((count, N_ROUNDS), np.int32)
    for rank in range(count):
        for step in range(N_ROUNDS):
            mine[round_target(rank, step), step] = rank
    theirs = mine[[partner(rank) for rank in range(count)]]
    late = np.broadcast_to(np.arange(count, rows, dtype=np.int32), (count, rows - count))
    order = np.concatenate([mine, theirs, late], axis=1)
    place = np.arange(rows)[None, :, None] == order[:, None, :]
    select = np.concatenate([mine, late], axis=1)[:, :, None] == np.arange(rows)[None, None, :]
    return np.concatenate([mine, theirs], axis=1), place, select


def run_copies(copies):
    for copy in copies:
        copy.start()
    for copy in copies:
        copy.wait()


def extract_kernel(steps, meta_ref, cache_ref, *rest):
    outs, (held, in_sem, out_sem) = rest[: len(steps)], rest[len(steps) :]
    rank = meta_ref[0]
    high, low = rank // NZ, rank % NZ
    sign = 1 - 2 * (low % 2)
    loads, stores = [], []
    for step, (shift, flip) in enumerate([ROUNDS[step] for step in steps]):
        target = (high + flip) % 2 * NZ + (low + NZ + sign * shift) % NZ
        columns = pl.ds(pl.multiple_of(target // 2 * HD, HD), HD)
        loads.append(
            pltpu.make_async_copy(cache_ref.at[:, :, columns], held.at[step], in_sem.at[step])
        )
        stores.append(pltpu.make_async_copy(held.at[step], outs[step], out_sem.at[step]))
    for load in loads:
        load.start()
    for load, store in zip(loads, stores):
        load.wait()
        store.start()
    for store in stores:
        store.wait()


def extract(steps, meta, cache):
    block = (2, cache.shape[1], HD)
    return pl.pallas_call(
        functools.partial(extract_kernel, steps),
        out_shape=[jax.ShapeDtypeStruct(block, cache.dtype)] * len(steps),
        in_specs=[SMEM, ANY],
        out_specs=[ANY] * len(steps),
        scratch_shapes=[
            pltpu.VMEM((len(steps),) + block, cache.dtype),
            pltpu.SemaphoreType.DMA((len(steps),)),
            pltpu.SemaphoreType.DMA((len(steps),)),
        ],
        compiler_params=pltpu.CompilerParams(vmem_limit_bytes=60 * MIB),
        name="extract",
    )(meta, cache)


def place_kernel(offset, count, n_out, index_ref, *rest):
    blocks, out_ref, sem = rest[:count], rest[-1 - n_out], rest[-1]
    run_copies([
        pltpu.make_async_copy(blocks[i], out_ref.at[index_ref[offset + i]], sem.at[i])
        for i in range(count)
    ])


def place(index, offset, blocks, rows, base=None, ready=None, carry=()):
    count = len(blocks)
    out = [jax.ShapeDtypeStruct((rows,) + blocks[0].shape, blocks[0].dtype)]
    operands, aliases = [], {}
    if base is not None:
        aliases[1 + count] = 0
        operands.append(base)
    if ready is not None:
        operands.append(ready)
    for array in carry:
        aliases[1 + count + len(operands)] = len(out)
        operands.append(array)
        out.append(jax.ShapeDtypeStruct(array.shape, array.dtype))
    return pl.pallas_call(
        functools.partial(place_kernel, offset, count, len(out)),
        out_shape=out,
        in_specs=[SMEM] + [VMEM] * count + [ANY] * len(operands),
        out_specs=[ANY] * len(out),
        scratch_shapes=[pltpu.SemaphoreType.DMA((count,))],
        input_output_aliases=aliases,
        compiler_params=pltpu.CompilerParams(vmem_limit_bytes=16 * MIB),
        name="place",
    )(index, *blocks, *operands)


def attend_kernel(first, heads, scale, len_ref, rows_ref, *rest):
    n_out = heads // 2
    blocks, outs = rest[: -5 - n_out], rest[-5 - n_out : -5]
    q_ref, k_ref, v_ref, prob_ref, blend_ref = rest[-5:]
    count = q_ref.shape[0] // PAD

    def block(b, kind):
        return blocks[0][b, kind] if len(blocks) == 1 else blocks[b][kind]

    new = GROUP * HD
    picked = slice(first, first + count)
    for g in range(PAD):
        spread = pl.ds(g, count, stride=PAD)
        lane = min(g, heads - 1) * HD
        q_ref[spread, :] = rows_ref[picked, lane : lane + HD]
        k_ref[spread, :] = rows_ref[picked, new : new + HD]
        v_ref[spread, :] = rows_ref[picked, new + HD : new + 2 * HD]
    for b in range(count):
        rows = slice(b * PAD, (b + 1) * PAD)
        scores = lax.dot_general(
            q_ref[rows, :].astype(jnp.bfloat16),
            block(b, 0),
            (((1,), (1,)), ((), ())),
            preferred_element_type=jnp.float32,
        )
        live = lax.broadcasted_iota(jnp.int32, scores.shape, 1) < len_ref[b]
        prob_ref[rows, :] = jnp.where(live, scores * scale, -1e30)
    scores = prob_ref[...]
    own = jnp.sum(q_ref[...] * k_ref[...], axis=-1, keepdims=True) * scale
    top = jnp.maximum(jnp.max(scores, axis=-1, keepdims=True), own)
    weights = jnp.exp(scores - top)
    own_weight = jnp.exp(own - top)
    total = jnp.sum(weights, axis=-1, keepdims=True) + own_weight
    prob_ref[...] = weights / total
    own_prob = (own_weight / total).astype(jnp.bfloat16).astype(jnp.float32)
    fresh = own_prob * v_ref[...]
    for b in range(count):
        rows = slice(b * PAD, (b + 1) * PAD)
        blended = jnp.dot(
            prob_ref[rows, :].astype(jnp.bfloat16),
            block(b, 1),
            preferred_element_type=jnp.float32,
        )
        blend_ref[rows, :] = blended + fresh[rows, :]
    for g in range(heads):
        outs[g // 2][:, g % 2 * HD : (g % 2 + 1) * HD] = blend_ref[pl.ds(g, count, stride=PAD), :]


def attend(first, heads, lengths, table, blocks):
    span = blocks[0].shape[-2]
    count = lengths.shape[0]
    wide = pltpu.VMEM((count * PAD, HD), jnp.float32)
    return pl.pallas_call(
        functools.partial(attend_kernel, first, heads, 1.0 / math.sqrt(HD)),
        out_shape=[jax.ShapeDtypeStruct((count, 2 * HD), jnp.float32)] * (heads // 2),
        in_specs=[SMEM] + [VMEM] * (1 + len(blocks)),
        out_specs=[VMEM] * (heads // 2),
        scratch_shapes=[wide, wide, wide, pltpu.VMEM((count * PAD, span), jnp.float32), wide],
        compiler_params=pltpu.CompilerParams(vmem_limit_bytes=16 * MIB),
        name="attend",
    )(lengths, table, *blocks)


def owner(rank, far, near):
    return ((rank ^ near) & 9) | (far << 1)


def project_kernel(meta_ref, place_ref, kept_ref, traded_ref, res_ref, weight_ref, *outs):
    gathered = jnp.concatenate([kept_ref[...], traded_ref[...], res_ref[...]], axis=0)
    attn = jnp.dot(
        place_ref[...], gathered.astype(jnp.bfloat16), preferred_element_type=jnp.float32
    ).astype(jnp.bfloat16)
    rank = meta_ref[0]
    for near, out_ref in zip((0,) + NEAR, outs):
        for far in range(4):
            chunk = out_ref.shape[2]
            columns = pl.ds(pl.multiple_of(owner(rank, far, near) * chunk, chunk), chunk)
            out_ref[far] = jnp.dot(
                attn, weight_ref[:, columns], preferred_element_type=jnp.float32
            ).astype(out_ref.dtype)


def project(meta, order, kept, traded, res, weight, count):
    shape = (4, order.shape[0], weight.shape[1] // count)
    return pl.pallas_call(
        project_kernel,
        out_shape=[jax.ShapeDtypeStruct(shape, jnp.bfloat16)] * 4,
        in_specs=[SMEM] + [VMEM] * 5,
        out_specs=[VMEM] * 4,
        compiler_params=pltpu.CompilerParams(vmem_limit_bytes=24 * MIB),
        name="project",
    )(meta, order, kept, traded, res, weight)


def near_kernel(*refs):
    parts, out_ref = refs[:4], refs[4]
    for far in range(4):
        summed = parts[0][far].astype(jnp.float32)
        for part in parts[1:]:
            summed = summed + part[far].astype(jnp.float32)
        out_ref[far] = summed.astype(out_ref.dtype)


def near_sum(parts):
    return pl.pallas_call(
        near_kernel,
        out_shape=jax.ShapeDtypeStruct(parts[0].shape, parts[0].dtype),
        in_specs=[VMEM] * 4,
        out_specs=VMEM,
        compiler_params=pltpu.CompilerParams(vmem_limit_bytes=16 * MIB),
        name="near_sum",
    )(*parts)


def far_kernel(meta_ref, *refs):
    parts, residual_ref, out_ref = refs[:4], refs[4], refs[5]
    chunk = out_ref.shape[2]
    for far in range(4):
        one, two, three, four = [part[far].astype(jnp.float32) for part in parts]
        summed = (one + two) + (three + four)
        columns = pl.ds(pl.multiple_of(owner(meta_ref[0], far, 0) * chunk, chunk), chunk)
        own = residual_ref[:, columns].astype(jnp.float32)
        out_ref[far] = (own + summed).astype(out_ref.dtype)


def far_sum(meta, parts, residual):
    return pl.pallas_call(
        far_kernel,
        out_shape=jax.ShapeDtypeStruct(parts[0].shape, residual.dtype),
        in_specs=[SMEM] + [VMEM] * 5,
        out_specs=VMEM,
        compiler_params=pltpu.CompilerParams(vmem_limit_bytes=16 * MIB),
        name="far_sum",
    )(meta, *parts, residual)


def finish_kernel(offset, count, meta_ref, index_ref, *rest):
    parts, blocks = rest[:4], rest[4 : 4 + count]
    mixed_ref, out_ref, sem = rest[-3:]
    copies = [
        pltpu.make_async_copy(blocks[i], out_ref.at[index_ref[offset + i]], sem.at[i])
        for i in range(count)
    ]
    for copy in copies:
        copy.start()
    rank = meta_ref[0]
    for near, part in zip((0,) + NEAR, parts):
        chunk = part.shape[2]
        for far in range(4):
            columns = pl.ds(pl.multiple_of(owner(rank, far, near) * chunk, chunk), chunk)
            mixed_ref[0, :, columns] = part[far]
    for copy in copies:
        copy.wait()


def finish(meta, index, parts, tp_count, offset, blocks, base):
    _, rows, chunk = parts[0].shape
    count = len(blocks)
    return pl.pallas_call(
        functools.partial(finish_kernel, offset, count),
        out_shape=[
            jax.ShapeDtypeStruct((1, rows, tp_count * chunk), parts[0].dtype),
            jax.ShapeDtypeStruct(base.shape, base.dtype),
        ],
        in_specs=[SMEM] * 2 + [VMEM] * (4 + count) + [ANY],
        out_specs=[VMEM, ANY],
        scratch_shapes=[pltpu.SemaphoreType.DMA((count,))],
        input_output_aliases={6 + count: 1},
        compiler_params=pltpu.CompilerParams(vmem_limit_bytes=16 * MIB),
        name="finish",
    )(meta, index, *parts, *blocks, base)


def hop(value, inst_count, tp_count, target):
    half = inst_count // 2
    pairs = [
        (i * tp_count + t, (i + half) % inst_count * tp_count + target(t))
        for i in range(inst_count)
        for t in range(tp_count)
    ]
    return lax.ppermute(value, ("inst", "tp"), pairs)


def after(value, others):
    return lax.optimization_barrier((value, *others))[0] if others else value


def swap(value, tp_count, bits=1):
    return lax.ppermute(value, "tp", [(t, t ^ bits) for t in range(tp_count)])


def on_device(source_cache, resident_cache, new_kv, queries, residual, lengths, out_weight):
    tp_count = lax.axis_size("tp")
    inst_count = lax.axis_size("inst")
    rank = lax.axis_index("tp")
    rows = queries.shape[1]
    adopt = tp_count
    chunk = out_weight.shape[1] // tp_count
    meta = rank.reshape(1).astype(jnp.int32)


    def send(step, block):
        return hop(block, inst_count, tp_count, lambda t: round_target(t, step))

    handed = hop(lengths[0], inst_count, tp_count, lambda t: t)
    other_q = swap(queries[0], tp_count)
    first = (4, 0)
    rest = tuple(step for step in range(N_ROUNDS) if step not in first)
    sent = dict(zip(first, extract(first, meta, source_cache[0, 0])))
    sent.update(zip(rest, extract(rest, meta, source_cache[0, 0])))
    sent = [
        sent[step] if step in first else after(sent[step], [handed, other_q])
        for step in range(N_ROUNDS)
    ]
    arrived = [send(step, sent[step]) for step in range(N_ROUNDS)]

    index, order, select = tables(tp_count, rows)
    index = lax.dynamic_index_in_dim(jnp.asarray(index), rank, keepdims=False)
    order = lax.dynamic_index_in_dim(jnp.asarray(order, jnp.bfloat16), rank, keepdims=False)
    select = lax.dynamic_index_in_dim(jnp.asarray(select, jnp.bfloat16), rank, keepdims=False)
    mine = index[:N_ROUNDS]
    fresh = lax.dynamic_slice_in_dim(new_kv[0], rank // 2 * HD, HD, axis=2)
    table = jnp.concatenate([queries[0], other_q, fresh.reshape(rows, 2 * HD)], axis=1)
    table = jnp.dot(select, table, preferred_element_type=jnp.float32)
    hit = mine[:, None] == jnp.arange(rows, dtype=jnp.int32)[None, :]
    adopt_len = jnp.sum(jnp.where(hit, handed[None, :], 0), axis=1)
    (res,) = attend(N_ROUNDS, 2, lengths[0, adopt:], table, [resident_cache[0, 0]])

    passed = [swap(block, tp_count) for block in arrived[:EARLY]]
    table = after(table, [*passed, res])
    kept, traded = attend(0, GROUP, adopt_len, table, arrived)

    def pass_on(ready, count):
        for _ in range(count):
            block = after(arrived[len(passed)], [ready])
            passed.append(swap(block, tp_count))

    traded = swap(traded, tp_count)
    parts = project(meta, order, kept, traded, res, out_weight, tp_count)
    pass_on(parts[0], 1)
    parts = [parts[0]] + [swap(part, tp_count, bits) for part, bits in zip(parts[1:], NEAR)]
    part = near_sum([after(parts[0], passed[:-1])] + parts[1:])
    pass_on(part, 1)
    parts = [part] + [swap(part, tp_count, bits) for bits in FAR]
    mixed = far_sum(meta, [after(part, passed[:-1])] + parts[1:], residual[0])
    pass_on(mixed, 1)
    parts = [mixed] + [swap(mixed, tp_count, bits) for bits in NEAR]
    (adopted,) = place(index, 0, (arrived + passed)[:PLACED], adopt, None, mixed)
    late = (arrived + passed)[PLACED:]
    mixed, adopted = finish(meta, index, parts, tp_count, PLACED, late, adopted)
    return (mixed, adopted[None, None])


def solution(mesh):
    in_specs = (
        P("inst", "tp", None, None, None),
        P("inst", "tp", None, None, None, None),
        P("inst", None, None, None),
        P("inst", None, "tp"),
        P("inst", None, None),
        P("inst", None),
        P("tp", None),
    )
    out_specs = (P("inst", None, None), P("inst", "tp", None, None, None, None))
    return jax.shard_map(
        on_device, mesh=mesh, in_specs=in_specs, out_specs=out_specs, check_vma=False
    )
```
